256 devices in a mesh: section: 4 (over z_hi), dp: 64 (over y, x, z_lo, core).
Axes of the slice: x: 4, y: 4, z: 8 (z_hi: 4, z_lo: 2; z = z_hi * 2 + z_lo), core: 2. Of those that a mesh axis runs over, the one named last changes fastest.
Arguments:
- activations: bfloat16 [4, 2, 4096, 2048], P('section', None, 'dp'), may hold values from -6 to 6
- routes: int32 [4, 2, 4096, 8], P('section', None, 'dp'), may hold values from 0 to 63, all different within a row; in each aligned block of 64 rows (0 to 63, 64 to 127, ..., all dimensions but the last counted through in order) at most 12 rows name the same one
- gates: bfloat16 [4, 2, 4096, 8], P('section', None, 'dp'), may hold values from 0.099609375 to 1
- hidden_cot: bfloat16 [4, 2, 64, 768, 768], P('section', None, 'dp'), may hold values from -1 to 1
- weight: bfloat16 [4, 64, 2048, 768], P('section', 'dp'), may hold values from -0.21875 to 0.21875
- top_cot: bfloat16 [2, 4096, 2048], P(None, 'dp'), may hold values from -1.1953125 to 1.1953125
Outputs:
- grad_sum: bfloat16 [4, 64, 2048, 768], P('section', 'dp')
- fisher: bfloat16 [4, 64, 2048, 768], P('section', 'dp')
- resid_grad: bfloat16 [4, 2, 4096, 2048], P('section', None, 'dp')
The draws below stay inside these ranges and needn't reach their ends.
Inputs may be any that keep to these rules, and one draw needn't show every extreme that they name: `routes`: each token names 8 different experts; among the tokens of one block of 64 of one section and micro-batch no expert is named by more than 12 tokens, a bound that some block reaches.
All inputs are finite; a program needn't handle non-finite values.
Results may differ from the reference program's by a relative error of at most 0.0054.
Values may be sent and summed in bfloat16 or wider, within the bound.
A program may use at most 128 MiB of HBM per device.

```python
import math
import jax
import jax.numpy as jnp
import numpy as np
from jax import lax

D = 2048
FW = 768
TOP = 8
BATCHES = 2
TOK_DEV = 64
SECTIONS = 4
EXPERTS = 64
TOKENS = 4096
CAP = 12
SLOTS = 768
N_DP = 64


def level_of(rng, extent, cuts, least, largest):
    gain = 1.0
    for axis_at, shards_of in cuts:
        draws = jax.random.uniform(jax.random.fold_in(jax.random.fold_in(rng, 6), axis_at), (shards_of,), jnp.float32, least / len(cuts), largest / len(cuts))
        gain = gain * jnp.repeat(jnp.exp(draws), extent[axis_at] // shards_of).reshape((-1,) + (1,) * (len(extent) - 1 - axis_at))
    return gain


def assign_block(stream_key, own, number, rows, amount, top, limit, skew):
    sequence = jax.random.permutation(stream_key, amount)
    heavy_load, ordinary = shares(amount, rows * top, limit, skew, True), shares(amount, rows * top, limit, skew, False)
    places = jnp.arange(amount)

    def named(lengths, offset_by):
        used = int((lengths > 0).sum())
        fixed = max(1, used // 4)
        shifted = fixed + (places - fixed + offset_by * (used - fixed)) % max(1, amount - fixed)
        return jnp.zeros((amount,), jnp.int32).at[sequence[jnp.where(places < fixed, places, shifted)]].set(jnp.asarray(lengths, jnp.int32))

    lengths = jnp.where(number % 4 == 0, named(heavy_load, number // 4), named(ordinary, number - number // 4 - 1))
    mixed = jax.random.permutation(jax.random.fold_in(own, 3), amount)
    giver, sink = mixed[0:amount // 2 * 2:2], mixed[1:amount // 2 * 2:2]
    room = jnp.minimum(lengths[giver] - 1, limit - lengths[sink]) // 2
    room = jnp.where((giver == sequence[0]) | (sink == sequence[0]) | (lengths[sink] == 0), 0, jnp.maximum(room, 0))
    shifted = jax.random.randint(jax.random.fold_in(own, 4), (amount // 2,), 0, 1 << 20) % (room + 1)
    lengths = lengths.at[giver].add(-shifted).at[sink].add(shifted)
    labels = jnp.searchsorted(jnp.cumsum(lengths), jnp.arange(rows * top), side="right").astype(jnp.int32)
    listing = labels.reshape(top, rows).T
    listing = listing[jax.random.permutation(jax.random.fold_in(own, 1), rows)]
    offset_by = jax.random.randint(jax.random.fold_in(own, 2), (rows, 1), 0, top)
    return jnp.take_along_axis(listing, (jnp.arange(top)[None, :] + offset_by) % top, axis=1)


def shares(amount, total, reach, slope, full):
    loads = [(1 << 20) // math.isqrt(rank ** slope) + 1 for rank in range(1, amount + 1)]
    largest = reach if full else min(reach, max(-(-total // amount), total * loads[0] // sum(loads)))
    least = 1 if total - largest >= amount - 1 else 0
    given, surplus = [largest] + [least] * (amount - 1), total - largest - least * (amount - 1)
    while surplus > 0:
        movable = [i for i in range(1, amount) if given[i] < largest] or [i for i in range(1, amount) if given[i] < reach]
        mass, remaining = sum([loads[i] for i in movable]), surplus
        for i in movable:
            extra = min(reach - given[i], max(1, remaining * loads[i] // mass), surplus)
            given[i] = given[i] + extra
            surplus = surplus - extra
    return np.array(given)


def gaussian(own_key, dims, deviation, bound, pieces=(), kind=jnp.bfloat16):
    level = level_of(own_key, dims, pieces, -0.22, 0.18) if pieces else 1.0
    array = jax.random.normal(own_key, dims, jnp.float32) * deviation * level
    return jnp.minimum(jnp.maximum(array, -bound), bound).astype(kind)


def setup_inputs(seed: int = 0) -> dict:
    splits = jax.random.split(jax.random.key(seed), 7)
    activations = gaussian(splits[0], (SECTIONS, BATCHES, TOKENS, D), 1.0, 6.0, ((0, 4), (2, 64)))
    routes_keys = jax.random.split(jax.random.fold_in(splits[1], 1), SECTIONS * BATCHES * TOKENS // TOK_DEV)
    routes_turns = jax.random.permutation(jax.random.fold_in(splits[1], 3), SECTIONS * BATCHES * TOKENS // TOK_DEV)
    routes = jax.vmap(lambda own, number: assign_block(jax.random.fold_in(splits[1], 2), own, number, TOK_DEV, EXPERTS, TOP, CAP, 2))(routes_keys, routes_turns).reshape((SECTIONS, BATCHES, TOKENS, TOP))
    gates = jnp.clip(0.099609375 + 0.9003906 * jax.random.uniform(splits[2], (SECTIONS, BATCHES, TOKENS, TOP), jnp.float32) ** level_of(splits[2], (SECTIONS, BATCHES, TOKENS, TOP), ((0, 4), (2, 64)), -0.2, 0.2), 0.099609375, 1.0).astype(jnp.bfloat16)
    hidden_cot = gaussian(splits[3], (SECTIONS, BATCHES, EXPERTS, SLOTS, FW), 0.15, 1.0, ((0, 4), (2, 64)))
    weight = gaussian(splits[4], (SECTIONS, EXPERTS, D, FW), FW ** -0.5, 0.21875, ((0, 4), (1, 64)))
    top_cot = gaussian(splits[5], (BATCHES, TOKENS, D), 0.2, 1.1953125, ((1, 64),))
    return {"activations": activations, "routes": routes, "gates": gates, "hidden_cot": hidden_cot, "weight": weight, "top_cot": top_cot}


def slot_positions(block_routes):
    flat_ids = block_routes.reshape(-1)
    onehot = (flat_ids[:, None] == jnp.arange(EXPERTS, dtype=jnp.int32)[None, :]).astype(jnp.int32)
    earlier = jnp.cumsum(onehot, axis=0) - onehot
    return flat_ids, jnp.sum(earlier * onehot, axis=1).astype(jnp.int32)


def slot_tables(route_ids, gate_vals):
    blocks = route_ids.reshape(N_DP, TOK_DEV, TOP)
    flat_ids, position = jax.vmap(slot_positions)(blocks)
    source = jnp.arange(N_DP, dtype=jnp.int32)[:, None]
    target = (flat_ids * SLOTS + source * CAP + position).reshape(-1)
    pair = jnp.arange(TOK_DEV * TOP, dtype=jnp.int32)[None, :] // TOP
    token_ids = (source * TOK_DEV + pair).reshape(-1)
    table = jnp.zeros((EXPERTS * SLOTS,), jnp.int32).at[target].set(token_ids + 1)
    gate_table = jnp.zeros((EXPERTS * SLOTS,), jnp.float32).at[target].set(gate_vals.reshape(-1).astype(jnp.float32))
    return table, gate_table


def reference(activations, routes, gates, hidden_cot, weight, top_cot):
    grad_list, fisher_list, comb_list = [], [], []
    for section_index in range(SECTIONS):
        grad_total = jnp.zeros((EXPERTS, D, FW), jnp.float32)
        fisher_total = jnp.zeros((EXPERTS, D, FW), jnp.float32)
        section_comb = []
        for batch_index in range(BATCHES):
            table, gate_table = slot_tables(routes[section_index, batch_index], gates[section_index, batch_index])
            features = activations[section_index, batch_index]

            def per_expert(item):
                table_row, gate_row, cot_rows, expert_weight = item
                picked = features[jnp.maximum(table_row - 1, 0)]
                expert_rows = jnp.where(table_row[:, None] > 0, picked, jnp.zeros((), jnp.bfloat16))
                scaled = (gate_row[:, None] * cot_rows.astype(jnp.float32)).astype(jnp.bfloat16)
                partial_value = jnp.dot(expert_rows.T, scaled, preferred_element_type=jnp.float32)
                back_rows = jnp.dot(scaled, expert_weight.T, preferred_element_type=jnp.float32).astype(jnp.bfloat16)
                return partial_value, back_rows

            partial_value, back_rows = lax.map(per_expert, (table.reshape(EXPERTS, SLOTS), gate_table.reshape(EXPERTS, SLOTS), hidden_cot[section_index, batch_index], weight[section_index]))
            grad_total = grad_total + partial_value
            fisher_total = fisher_total + partial_value * partial_value
            target = jnp.where(table > 0, table - 1, TOKENS)
            combined = jnp.zeros((TOKENS, D), jnp.float32).at[target].add(back_rows.reshape(-1, D).astype(jnp.float32), mode="drop")
            section_comb.append(combined)
        grad_list.append(grad_total.astype(jnp.bfloat16))
        fisher_list.append(fisher_total.astype(jnp.bfloat16))
        comb_list.append(jnp.stack(section_comb))
    resid_list = []
    running = top_cot.astype(jnp.float32)
    for section_index in range(SECTIONS - 1, -1, -1):
        running = running + comb_list[section_index]
        resid_list.append(running.astype(jnp.bfloat16))
    resid_list = resid_list[::-1]
    return jnp.stack(grad_list), jnp.stack(fisher_list), jnp.stack(resid_list)
```

```python
import jax
import jax.numpy as jnp
from jax import lax
from jax.experimental import pallas as pl
from jax.experimental.pallas import tpu as pltpu
from jax.sharding import PartitionSpec as P

MESH = pl.DeviceIdType.MESH
M = 2
T = 64
D = 2048
F = 768
E = 64
CAP = 12
NB = 8
NI = 8
ROWS = NB * CAP
NC = 4
CW = D // NC
NT = (((1,), (1,)), ((), ()))
TN = (((0,), (0,)), ((), ()))
F32 = jnp.float32
BF16 = jnp.bfloat16


def dot(a, b, dims=(((1,), (0,)), ((), ()))):
    return lax.dot_general(a, b, dims, preferred_element_type=F32)


def iota(shape, dim):
    return lax.broadcasted_iota(jnp.int32, shape, dim)


def kernel(
    act, routes, gates, hcot, wgt, top,
    grad, fish, resid,
    meta, tok, hh, hht, gsend, gin, hc, wv, tv, scaled, bsend, bin_, rows,
    pown, psend, rin, ssend, sin, csend, cin, rstage, gstage, fstage,
    lsem, osem, mz_s, mz_r, tz_s, tz_r, mu_s, mu_r, tu_s, tu_r, g_s, g_r,
    r1_s, r1_r, r2_s, r2_r, r3_s, r3_r, d3_s, d3_r, ch_s, ch_r,
):
    sec = lax.axis_index("section")
    me = lax.axis_index("dp")
    y, x, z, c = me // 16, (me // 4) % 4, (me // 2) % 2, me % 2

    def index(yy, xx, zz, cc):
        return ((yy * 4 + xx) * 2 + zz) * 2 + cc

    def peer_u(m, du):
        if m == 0:
            return index((y + du) % 4, x, z, c)
        return index(y, (x + du) % 4, z, c)

    def peer_v(m, dv, dc):
        if m == 0:
            return index(y, (x + dv) % 4, z, (c + dc) % 2)
        return index((y + dv) % 4, x, z, (c + dc) % 2)

    peer_z = index(y, x, 1 - z, c)

    def remote(src, dst, ssem, rsem, dev):
        return pltpu.make_async_remote_copy(
            src_ref=src, dst_ref=dst, send_sem=ssem, recv_sem=rsem,
            device_id={"dp": dev}, device_id_type=MESH)

    act_cp = [pltpu.make_async_copy(act.at[m], tok.at[m, 0], lsem.at[m]) for m in range(M)]
    hc_cp = pltpu.make_async_copy(hcot, hc, lsem.at[2])
    w_cp = pltpu.make_async_copy(wgt, wv, lsem.at[3])
    t_cp = pltpu.make_async_copy(top, tv, lsem.at[4])
    for cp in act_cp + [hc_cp, w_cp, t_cp]:
        cp.start()

    bar = pltpu.get_barrier_semaphore()
    peers = [peer_z, index(y, x, z, 1 - c)]
    for m in range(M):
        for dv in range(1, 4):
            for dc in range(2):
                peers.append(peer_v(m, dv, dc))
    for p in peers:
        pl.semaphore_signal(bar, inc=1, device_id={"dp": p}, device_id_type=MESH)
    for ds in (1, 3):
        pl.semaphore_signal(bar, inc=1, device_id={"section": (sec + ds) % 4}, device_id_type=MESH)

    lane = iota((T, 128), 1)
    expert = lane & (E - 1)
    lower = (iota((T, T), 0) > iota((T, T), 1)).astype(F32).astype(BF16)
    for m in range(M):
        r = routes[m]
        g = gates[m].astype(F32)
        named = jnp.zeros((T, 128), F32)
        gate = jnp.zeros((T, 128), F32)
        for k in range(8):
            eq = r[:, k:k + 1] == expert
            named = jnp.where(eq, 1.0, named)
            gate = jnp.where(eq, g[:, k:k + 1], gate)
        pos = dot(lower, named.astype(BF16))
        meta[m, 0] = jnp.where(lane < E, jnp.where(named > 0.0, pos, 128.0), gate).astype(BF16)

    pl.semaphore_wait(bar, len(peers) + 2)

    mz = [remote(meta.at[m, 0], meta.at[m, 4], mz_s.at[m], mz_r.at[m], peer_z) for m in range(M)]
    tz = [remote(tok.at[m, 0], tok.at[m, 4], tz_s.at[m], tz_r.at[m], peer_z) for m in range(M)]
    mu = {}
    tu = {}
    for m in range(M):
        for zz in range(2):
            for du in range(1, 4):
                far = zz * 4 + (4 - du) % 4
                k = (m * 2 + zz) * 3 + du - 1
                mu[m, zz, du] = remote(meta.at[m, zz * 4], meta.at[m, far], mu_s.at[k], mu_r.at[k], peer_u(m, du))
                tu[m, zz, du] = remote(tok.at[m, zz * 4], tok.at[m, far], tu_s.at[k], tu_r.at[k], peer_u(m, du))
    for m in range(M):
        mz[m].start()
    for m in range(M):
        for du in range(1, 4):
            mu[m, 0, du].start()
    for m in range(M):
        act_cp[m].wait()
        tz[m].start()
        for du in range(1, 4):
            tu[m, 0, du].start()
    for m in range(M):
        mz[m].wait_recv()
        for du in range(1, 4):
            mu[m, 1, du].start()
    for m in range(M):
        for zz in range(2):
            for du in range(1, 4):
                mu[m, zz, du].wait_recv()

    def exchange_expert(m, i):
        dv, dc = i >> 1, i & 1
        if m == 0:
            return index(y, (x + dv) & 3, z, (c + dc) & 1)
        return index((y + dv) & 3, x, z, (c + dc) & 1)

    gcopy = {}
    for m in range(M):
        block = meta[m].reshape(NB * T, 128)
        l = iota((128, NI * ROWS), 1)
        i = (l * 683) >> 16
        sel = (iota((128, NI * ROWS), 0) == exchange_expert(m, i)).astype(F32).astype(BF16)
        l = iota((NB * T, NI * ROWS), 1)
        want = l - ((l * 683) >> 16) * ROWS - CAP * (iota((NB * T, NI * ROWS), 0) >> 6)
        hht[m] = (dot(block, sel) == want.astype(F32)).astype(F32).astype(BF16)
        r = iota((NI * ROWS, 128), 0)
        i = (r * 683) >> 16
        sel = (iota((NI * ROWS, 128), 1) == exchange_expert(m, i)).astype(F32).astype(BF16)
        r = iota((NI * ROWS, NB * T), 0)
        want = r - ((r * 683) >> 16) * ROWS - CAP * (iota((NI * ROWS, NB * T), 1) >> 6)
        hh[m] = (dot(sel, block, NT) == want.astype(F32)).astype(F32).astype(BF16)
        l = iota((128, NI * 128), 1)
        p = iota((128, NI * 128), 0)
        e = exchange_expert(m, l >> 7)
        sel = (p == e).astype(F32).astype(BF16)
        gsel = (p == e + E).astype(F32).astype(BF16)
        want = (iota((NB * T, NI * 128), 1) & 127) - CAP * (iota((NB * T, NI * 128), 0) >> 6)
        hit = dot(block, sel) == want.astype(F32)
        grow = jnp.sum(jnp.where(hit, dot(block, gsel), 0.0), axis=0, keepdims=True)
        for i in range(NI):
            row = jnp.broadcast_to(grow[:, i * 128:(i + 1) * 128], (16, 128)).astype(BF16)
            if i == 0:
                gin[m, 0] = row
                continue
            gsend[m, i] = row
            k = m * 7 + i - 1
            gcopy[m, i] = remote(gsend.at[m, i], gin.at[m, i], g_s.at[k], g_r.at[k], peer_v(m, i // 2, i % 2))
            gcopy[m, i].start()

    for m in range(M):
        tz[m].wait_recv()
        for du in range(1, 4):
            tu[m, 1, du].start()

    hc_cp.wait()
    for m in range(M):
        for i in range(1, NI):
            gcopy[m, i].wait_recv()
        for i in range(NI):
            dv, dc = i // 2, i % 2
            eye = iota((ROWS, 128), 0) == iota((ROWS, 128), 1)
            gcol = jnp.sum(jnp.where(eye, gin[m, i][0:1].astype(F32), 0.0), axis=1, keepdims=True)
            r = iota((ROWS, F), 0)
            b = (r * 171) >> 11
            q = r - b * CAP
            zs = (z + (b >> 2)) & 1
            us = b & 3
            if m == 0:
                j = index((y + us) & 3, (x + 4 - dv) % 4, zs, (c + dc) % 2)
            else:
                j = index((y + 4 - dv) % 4, (x + us) & 3, zs, (c + dc) % 2)
            pick = jnp.where(iota((ROWS, F), 1) == j * CAP + q, gcol, 0.0).astype(BF16)
            scaled[m, i * ROWS:(i + 1) * ROWS] = dot(pick, hc[m]).astype(BF16)

    w_cp.wait()
    r1 = {}
    d3 = {}
    for n in range(NC):
        for m in range(M):
            for i in range(1, NI):
                dv, dc = i // 2, i % 2
                k = (m * NC + n) * 7 + i - 1
                part = pl.ds(i * ROWS, ROWS)
                r1[m, n, i] = remote(bsend.at[m, n, part], bin_.at[m, n, part], r1_s.at[k], r1_r.at[k],
                                     peer_v(m, (4 - dv) % 4, dc))
                d3[m, n, i] = remote(bsend.at[m, n, part], rows.at[m, n, part], d3_s.at[k], d3_r.at[k],
                                     peer_v(m, dv, dc))
    for n in range(NC):
        for m in range(M):
            back = dot(scaled[m], wv[n * CW:(n + 1) * CW], NT).astype(BF16)
            bin_[m, n, 0:ROWS] = back[0:ROWS]
            bsend[m, n, ROWS:] = back[ROWS:]
            for i in range(1, NI):
                r1[m, n, i].start()

    for m in range(M):
        for zz in range(2):
            for du in range(1, 4):
                tu[m, zz, du].wait_recv()
    t_cp.wait()

    r2 = {}
    r3 = {}
    for n in range(NC):
        for m in range(M):
            k = m * NC + n
            r2[m, n] = remote(psend.at[m, n], rin.at[m, n], r2_s.at[k], r2_r.at[k], peer_z)
            for du in range(1, 4):
                k = (m * NC + n) * 3 + du - 1
                r3[m, n, du] = remote(ssend.at[m, n, du - 1], sin.at[m, n, du - 1], r3_s.at[k], r3_r.at[k],
                                      peer_u(m, du))
    ch = [pltpu.make_async_remote_copy(
        src_ref=csend.at[n], dst_ref=cin.at[n], send_sem=ch_s.at[n], recv_sem=ch_r.at[n],
        device_id={"section": (sec + 3) % 4}, device_id_type=MESH) for n in range(NC)]

    def combine(n):
        for m in range(M):
            for i in range(1, NI):
                r1[m, n, i].wait_recv()
            part = dot(hht[m], bin_[m, n])
            psend[m, n] = part[4 * T:].astype(BF16)
            r2[m, n].start()
            pown[m, n] = part[:4 * T]

    def send_rows(n):
        for m in range(M):
            for i in range(1, NI):
                r1[m, n, i].wait_send()
            gathered = tok[m, :, :, n * CW:(n + 1) * CW].reshape(NB * T, CW)
            out = dot(hh[m], gathered).astype(BF16)
            rows[m, n, 0:ROWS] = out[0:ROWS]
            bsend[m, n, ROWS:] = out[ROWS:]
            for i in range(1, NI):
                d3[m, n, i].start()

    def spread(n):
        for m in range(M):
            r2[m, n].wait_recv()
            total = pown[m, n] + rin[m, n].astype(F32)
            for du in range(1, 4):
                ssend[m, n, du - 1] = total[du * T:(du + 1) * T].astype(BF16)
                r3[m, n, du].start()
            pown[m, n, 0:T] = total[0:T]

    outs = {}

    def weights(n):
        slot = n % 2
        if n >= 2:
            for cp in outs[n - 2]:
                cp.wait()
        for m in range(M):
            for i in range(1, NI):
                d3[m, n, i].wait_recv()
        p0 = dot(rows[0, n], scaled[0], TN)
        p1 = dot(rows[1, n], scaled[1], TN)
        gstage[slot] = (p0 + p1).astype(BF16)
        fstage[slot] = (p0 * p0 + p1 * p1).astype(BF16)
        cut = pl.ds(n * CW, CW)
        outs[n] = [pltpu.make_async_copy(gstage.at[slot], grad.at[cut], osem.at[slot]),
                   pltpu.make_async_copy(fstage.at[slot], fish.at[cut], osem.at[2 + slot])]
        for cp in outs[n]:
            cp.start()

    @pl.when(sec == 3)
    def _():
        cin[...] = jnp.zeros_like(cin)

    def chain(n):
        for m in range(M):
            for du in range(1, 4):
                r3[m, n, du].wait_recv()

        @pl.when(sec < 3)
        def _():
            ch[n].wait_recv()

        for m in range(M):
            total = pown[m, n, 0:T] + cin[n, m].astype(F32)
            for du in range(1, 4):
                total = total + sin[m, n, du - 1].astype(F32)
            csend[n, m] = total.astype(BF16)
            cut = pl.ds(n * CW, CW)
            rstage[m, :, cut] = (tv[m, :, cut].astype(F32) + total).astype(BF16)

        @pl.when(sec > 0)
        def _():
            ch[n].start()

    for step in range(NC + 2):
        if step < NC:
            combine(step)
            send_rows(step)
        if 0 <= step - 1 < NC:
            spread(step - 1)
            weights(step - 1)
        if 0 <= step - 2 < NC:
            chain(step - 2)

    out_r = pltpu.make_async_copy(rstage, resid, lsem.at[5])
    out_r.start()
    for m in range(M):
        mz[m].wait_send()
        tz[m].wait_send()
        for i in range(1, NI):
            gcopy[m, i].wait_send()
        for zz in range(2):
            for du in range(1, 4):
                mu[m, zz, du].wait_send()
                tu[m, zz, du].wait_send()
        for n in range(NC):
            for i in range(1, NI):
                d3[m, n, i].wait_send()
            r2[m, n].wait_send()
            for du in range(1, 4):
                r3[m, n, du].wait_send()

    @pl.when(sec > 0)
    def _():
        for n in range(NC):
            ch[n].wait_send()

    for n in range(NC - 2, NC):
        for cp in outs[n]:
            cp.wait()
    out_r.wait()


def fused(act, routes, gates, hcot, wgt, top):
    hbm = pl.BlockSpec(memory_space=pl.ANY)
    vmem = pl.BlockSpec(memory_space=pltpu.VMEM)
    sem = pltpu.SemaphoreType.DMA
    v = pltpu.VMEM
    pairs = [M, M, M * 6, M * 6, M * 7, M * NC * 7, M * NC, M * NC * 3, M * NC * 7, NC]
    sems = [sem((6,)), sem((4,))]
    for n in pairs:
        sems += [sem((n,)), sem((n,))]
    return pl.pallas_call(
        kernel,
        out_shape=(
            jax.ShapeDtypeStruct((D, F), BF16),
            jax.ShapeDtypeStruct((D, F), BF16),
            jax.ShapeDtypeStruct((M, T, D), BF16),
        ),
        in_specs=[hbm, vmem, vmem, hbm, hbm, hbm],
        out_specs=(hbm, hbm, hbm),
        scratch_shapes=[
            v((M, NB, T, 128), BF16),
            v((M, NB, T, D), BF16),
            v((M, NI * ROWS, NB * T), BF16),
            v((M, NB * T, NI * ROWS), BF16),
            v((M, NI, 16, 128), BF16),
            v((M, NI, 16, 128), BF16),
            v((M, F, F), BF16),
            v((D, F), BF16),
            v((M, T, D), BF16),
            v((M, NI * ROWS, F), BF16),
            v((M, NC, NI * ROWS, CW), BF16),
            v((M, NC, NI * ROWS, CW), BF16),
            v((M, NC, NI * ROWS, CW), BF16),
            v((M, NC, 4 * T, CW), F32),
            v((M, NC, 4 * T, CW), BF16),
            v((M, NC, 4 * T, CW), BF16),
            v((M, NC, 3, T, CW), BF16),
            v((M, NC, 3, T, CW), BF16),
            v((NC, M, T, CW), BF16),
            v((NC, M, T, CW), BF16),
            v((M, T, D), BF16),
            v((2, CW, F), BF16),
            v((2, CW, F), BF16),
        ] + sems,
        compiler_params=pltpu.CompilerParams(
            collective_id=0, has_side_effects=True, vmem_limit_bytes=62 * 2**20),
        cost_estimate=pl.CostEstimate(flops=18 * 10**9, bytes_accessed=26 * 10**6, transcendentals=0),
        name="expert_backward",
    )(act, routes, gates, hcot, wgt, top)


def shards(activations, routes, gates, hidden_cot, weight, top_cot):
    grad, fish, resid = fused(
        activations[0], routes[0], gates[0], hidden_cot[0, :, 0], weight[0, 0], top_cot)
    return grad[None, None], fish[None, None], resid[None]


def solution(mesh):
    return jax.shard_map(
        shards,
        mesh=mesh,
        in_specs=(
            P("section", None, "dp", None),
            P("section", None, "dp", None),
            P("section", None, "dp", None),
            P("section", None, "dp", None, None),
            P("section", "dp", None, None),
            P(None, "dp", None),
        ),
        out_specs=(
            P("section", "dp", None, None),
            P("section", "dp", None, None),
            P("section", None, "dp", None),
        ),
        check_vma=False,
    )
```

```python
import jax
import jax.numpy as jnp
from jax import lax
from jax.experimental import pallas as pl
from jax.experimental.pallas import tpu as pltpu
from jax.sharding import PartitionSpec as P

MESH = pl.DeviceIdType.MESH
M = 2
T = 64
D = 2048
F = 768
E = 64
CAP = 12
NB = 8
NI = 8
ROWS = NB * CAP
NC = 4
CW = D // NC
NT = (((1,), (1,)), ((), ()))
TN = (((0,), (0,)), ((), ()))
F32 = jnp.float32
BF16 = jnp.bfloat16


def dot(a, b, dims=(((1,), (0,)), ((), ()))):
    return lax.dot_general(a, b, dims, preferred_element_type=F32)


def iota(shape, dim):
    return lax.broadcasted_iota(jnp.int32, shape, dim)


class Copy:
    def __init__(self, copy, started):
        self.copy, self.started = copy, started
        self.sent = self.received = False

    def start(self):
        self.copy.start()
        self.started.append(self)

    def wait_recv(self):
        if not self.received:
            self.copy.wait_recv()
        self.received = True

    def wait_send(self):
        if not self.sent:
            self.copy.wait_send()
        self.sent = True


def kernel(
    act, routes, gates, hcot, wgt, top,
    grad, fish, resid,
    slot, meta, tok, hh, hht, gsend, gin, pick, hc, wv, tv, scaled, bsend, bin_, rows,
    pown, psend, rin, ssend, sin, lsend, lin, csend, cin, rstage, gstage, fstage,
    lsem, osem, tz_s, tz_r, su_s, su_r, mu_s, mu_r, tu_s, tu_r, tf_s, tf_r, g_s, g_r,
    r1_s, r1_r, r2_s, r2_r, r3_s, r3_r, d3_s, d3_r, ch_s, ch_r,
):
    sec = lax.axis_index("section")
    me = lax.axis_index("dp")
    y, x, z, c = me // 16, (me // 4) % 4, (me // 2) % 2, me % 2

    def index(yy, xx, zz, cc):
        return ((yy * 4 + xx) * 2 + zz) * 2 + cc

    def peer_u(m, du, dz=0):
        if m == 0:
            return index((y + du) % 4, x, (z + dz) % 2, c)
        return index(y, (x + du) % 4, (z + dz) % 2, c)

    def peer_v(m, dv, dc):
        if m == 0:
            return index(y, (x + dv) % 4, z, (c + dc) % 2)
        return index((y + dv) % 4, x, z, (c + dc) % 2)

    peer_z = index(y, x, 1 - z, c)

    started = []

    def remote(src, dst, ssem, rsem, dev):
        return Copy(pltpu.make_async_remote_copy(
            src_ref=src, dst_ref=dst, send_sem=ssem, recv_sem=rsem,
            device_id={"dp": dev}, device_id_type=MESH), started)

    act_cp = [pltpu.make_async_copy(act.at[m], tok.at[m, 0], lsem.at[m]) for m in range(M)]
    hc_cp = pltpu.make_async_copy(hcot, hc, lsem.at[2])
    w_cp = pltpu.make_async_copy(wgt, wv, lsem.at[3])
    t_cp = pltpu.make_async_copy(top, tv, lsem.at[4])
    for cp in act_cp + [hc_cp, w_cp, t_cp]:
        cp.start()

    bar = pltpu.get_barrier_semaphore()
    peers = [peer_z, index(y, x, z, 1 - c)]
    for du in range(1, 4):
        peers += [index((y + du) % 4, x, 1 - z, c), index(y, (x + du) % 4, 1 - z, c)]
    for m in range(M):
        for dv in range(1, 4):
            for dc in range(2):
                peers.append(peer_v(m, dv, dc))
    for p in peers:
        pl.semaphore_signal(bar, inc=1, device_id={"dp": p}, device_id_type=MESH)
    for ds in (1, 2, 3):
        pl.semaphore_signal(bar, inc=1, device_id={"section": (sec + ds) % 4}, device_id_type=MESH)

    expert = iota((128, T), 0) & (E - 1)
    lower = (iota((T, T), 0) > iota((T, T), 1)).astype(F32).astype(BF16)
    same = (iota((T, T), 0) == iota((T, T), 1)).astype(F32).astype(BF16)
    for m in range(M):
        r = routes[m]
        g = gates[m].astype(F32)
        named = jnp.zeros((128, T), F32)
        gate = jnp.zeros((128, T), F32)
        for k in range(8):
            eq = r[k:k + 1] == expert
            named = jnp.where(eq, 1.0, named)
            gate = jnp.where(eq, g[k:k + 1], gate)
        named = named.astype(BF16)
        pos = jnp.where(dot(same, named, NT) > 0.0, dot(lower, named, NT), 128.0)
        gate = dot(same, gate.astype(BF16), NT)
        meta[m, 0] = pos.astype(BF16)
        slots = [jnp.sum(jnp.where(pos == float(q), gate, 0.0), axis=0, keepdims=True) for q in range(CAP)]
        slots.append(jnp.zeros((16 - CAP, 128), F32))
        slot[m, 0] = jnp.concatenate(slots, axis=0).astype(BF16)

    pl.semaphore_wait(bar, len(peers) + 3)

    tz = [remote(tok.at[m, 0], tok.at[m, 4], tz_s.at[m], tz_r.at[m], peer_z) for m in range(M)]
    mu = {}
    su = {}
    tu = {}
    tf = {}
    for m in range(M):
        for zz in range(2):
            at = zz * 4
            for du in range(4):
                if zz or du:
                    k = m * 7 + zz * 4 + du - 1
                    su[m, zz, du] = remote(slot.at[m, 0], slot.at[m, at + (4 - du) % 4], su_s.at[k], su_r.at[k],
                                           peer_u(m, du, zz))
                    mu[m, zz, du] = remote(meta.at[m, 0], meta.at[m, at + (4 - du) % 4], mu_s.at[k], mu_r.at[k],
                                           peer_u(m, du, zz))
            for side, du in enumerate((1, 3)):
                k = (m * 2 + zz) * 2 + side
                half = pl.ds(side * (T // 2), T // 2)
                tu[m, zz, side] = remote(tok.at[m, at], tok.at[m, at + 4 - du], tu_s.at[k], tu_r.at[k], peer_u(m, du))
                tf[m, zz, side] = remote(tok.at[m, at + 4 - du, half], tok.at[m, at + 2, half],
                                         tf_s.at[k], tf_r.at[k], peer_u(m, du))

    def forward(zz):
        for m in range(M):
            for side in range(2):
                tu[m, zz, side].wait_recv()
                tf[m, zz, side].start()

    for at in su:
        su[at].start()
    for m in range(M):
        act_cp[m].wait()
        for side in range(2):
            tu[m, 0, side].start()
        tz[m].start()
    for at in su:
        su[at].wait_recv()

    def exchange_expert(m, i):
        dv, dc = i >> 1, i & 1
        if m == 0:
            return index(y, (x + dv) & 3, z, (c + dc) & 1)
        return index((y + dv) & 3, x, z, (c + dc) & 1)

    gcopy = {}
    for m in range(M):
        table = slot[m].reshape(NB * 16, 128)
        sel = (iota((16, 128), 1) == exchange_expert(m, iota((16, 128), 0) & 7)).astype(F32).astype(BF16)
        gsend[m] = dot(sel, table, NT).astype(BF16)
        for i in range(1, NI):
            k = m * 7 + i - 1
            gcopy[m, i] = remote(gsend.at[m], gin.at[m, i], g_s.at[k], g_r.at[k], peer_v(m, i // 2, i % 2))
            gcopy[m, i].start()

    def row_masks(m):
        block = meta[m].reshape(NB * T, 128)
        r = iota((NI * ROWS, 128), 0)
        i = (r * 683) >> 16
        sel = (iota((NI * ROWS, 128), 1) == exchange_expert(m, i)).astype(F32).astype(BF16)
        r = iota((NI * ROWS, NB * T), 0)
        want = r - ((r * 683) >> 16) * ROWS - CAP * (iota((NI * ROWS, NB * T), 1) >> 6)
        hh[m] = (dot(sel, block, NT) == want.astype(F32)).astype(F32).astype(BF16)

    for at in mu:
        mu[at].start()
    forward(0)
    for m in range(M):
        tz[m].wait_recv()
        for side in range(2):
            tu[m, 1, side].start()

    hc_cp.wait()
    r = iota((ROWS, 128), 0)
    b = (r * 171) >> 11
    place = (iota((ROWS, 128), 1) == b * 16 + r - b * CAP).astype(F32).astype(BF16)
    r = iota((ROWS, 1), 0)
    b = (r * 171) >> 11
    q = r - b * CAP
    zs = (z + (b >> 2)) & 1
    us = b & 3
    for m in range(M):
        for i in range(1, NI):
            gcopy[m, i].wait_recv()
        for i in range(NI):
            dv, dc = i // 2, i % 2
            got = gsend[m] if i == 0 else gin[m, i]
            gcol = dot(place, got, NT)[:, i:i + 1]
            if m == 0:
                j = index((y + us) & 3, (x + 4 - dv) % 4, zs, (c + dc) % 2)
            else:
                j = index((y + 4 - dv) % 4, (x + us) & 3, zs, (c + dc) % 2)
            pick[i * ROWS:(i + 1) * ROWS] = jnp.where(iota((ROWS, F), 1) == j * CAP + q, gcol, 0.0).astype(BF16)
        scaled[m] = dot(pick[...], hc[m]).astype(BF16)

    w_cp.wait()
    r1 = {}
    d3 = {}
    for n in range(NC):
        for m in range(M):
            for i in range(1, NI):
                dv, dc = i // 2, i % 2
                k = (m * NC + n) * 7 + i - 1
                part = pl.ds(i * ROWS, ROWS)
                r1[m, n, i] = remote(bsend.at[m, n, part], bin_.at[m, n, part], r1_s.at[k], r1_r.at[k],
                                     peer_v(m, (4 - dv) % 4, dc))
                d3[m, n, i] = remote(bsend.at[m, n, part], rows.at[m, n, part], d3_s.at[k], d3_r.at[k],
                                     peer_v(m, dv, dc))
    for n in range(NC):
        for m in range(M):
            back = dot(scaled[m], wv[n * CW:(n + 1) * CW], NT).astype(BF16)
            bin_[m, n, 0:ROWS] = back[0:ROWS]
            bsend[m, n, ROWS:] = back[ROWS:]
            for i in range(1, NI):
                r1[m, n, i].start()

    forward(1)
    for at in mu:
        mu[at].wait_recv()
    for m in range(M):
        block = meta[m].reshape(NB * T, 128)
        l = iota((128, NI * ROWS), 1)
        i = (l * 683) >> 16
        sel = (iota((128, NI * ROWS), 0) == exchange_expert(m, i)).astype(F32).astype(BF16)
        l = iota((NB * T, NI * ROWS), 1)
        want = l - ((l * 683) >> 16) * ROWS - CAP * (iota((NB * T, NI * ROWS), 0) >> 6)
        hht[m] = (dot(block, sel) == want.astype(F32)).astype(F32).astype(BF16)

    for m in range(M):
        row_masks(m)
    t_cp.wait()

    r2 = {}
    r3 = {}
    for m in range(M):
        n = NC - 1
        near = pl.ds(0, T)
        r2[m, n] = remote(psend.at[m, n, near], rin.at[m, n, near], r2_s.at[m * NC + n], r2_r.at[m * NC + n], peer_z)
        for du in range(1, 4):
            k = (m * NC + n) * 3 + du - 1
            r3[m, n, du] = remote(lsend.at[m, du - 1], lin.at[m, du - 1], r3_s.at[k], r3_r.at[k], peer_u(m, du))
    for n in range(NC - 1):
        for m in range(M):
            k = m * NC + n
            r2[m, n] = remote(psend.at[m, n], rin.at[m, n], r2_s.at[k], r2_r.at[k], peer_z)
            for du in range(1, 4):
                k = (m * NC + n) * 3 + du - 1
                r3[m, n, du] = remote(ssend.at[m, n, du - 1], sin.at[m, n, du - 1], r3_s.at[k], r3_r.at[k],
                                      peer_u(m, du))
    down = {(n, k, m): pltpu.make_async_remote_copy(
        src_ref=csend.at[n, m], dst_ref=cin.at[k - 1, n, m],
        send_sem=ch_s.at[(n * 3 + k - 1) * M + m], recv_sem=ch_r.at[(n * 3 + k - 1) * M + m],
        device_id={"section": (sec + 4 - k) % 4}, device_id_type=MESH)
        for n in range(NC) for k in range(1, 4) for m in range(M)}

    def combine(n):
        for m in range(M):
            for i in range(1, NI):
                r1[m, n, i].wait_recv()
            part = dot(hht[m], bin_[m, n])
            if n == NC - 1:
                for zz in range(2):
                    for du in range(4):
                        one = part[(zz * 4 + du) * T:(zz * 4 + du + 1) * T]
                        if du == 0:
                            pown[m, n, zz * T:(zz + 1) * T] = one
                        else:
                            lsend[m, du - 1, zz] = one.astype(BF16)
                for du in range(1, 4):
                    r3[m, n, du].start()
                continue
            psend[m, n] = part[4 * T:].astype(BF16)
            r2[m, n].start()
            pown[m, n] = part[:4 * T]

    def send_rows(n):
        for m in range(M):
            for i in range(1, NI):
                r1[m, n, i].wait_send()
            gathered = tok[m, :, :, n * CW:(n + 1) * CW].reshape(NB * T, CW)
            out = dot(hh[m], gathered).astype(BF16)
            rows[m, n, 0:ROWS] = out[0:ROWS]
            bsend[m, n, ROWS:] = out[ROWS:]
            for i in range(1, NI):
                d3[m, n, i].start()

    def spread(n):
        for m in range(M):
            if n == NC - 1:
                total = [pown[m, n, zz * T:(zz + 1) * T] for zz in range(2)]
                for du in range(1, 4):
                    r3[m, n, du].wait_recv()
                    total = [total[zz] + lin[m, du - 1, zz].astype(F32) for zz in range(2)]
                psend[m, n, 0:T] = total[1].astype(BF16)
                r2[m, n].start()
                pown[m, n, 0:T] = total[0]
                continue
            r2[m, n].wait_recv()
            total = pown[m, n] + rin[m, n].astype(F32)
            for du in range(1, 4):
                ssend[m, n, du - 1] = total[du * T:(du + 1) * T].astype(BF16)
                r3[m, n, du].start()
            pown[m, n, 0:T] = total[0:T]

    outs = {}

    def weights(n):
        turn = n % 2
        if n >= 2:
            for cp in outs[n - 2]:
                cp.wait()
        for m in range(M):
            for i in range(1, NI):
                d3[m, n, i].wait_recv()
        p0 = dot(rows[0, n], scaled[0], TN)
        p1 = dot(rows[1, n], scaled[1], TN)
        gstage[turn] = (p0 + p1).astype(BF16)
        fstage[turn] = (p0 * p0 + p1 * p1).astype(BF16)
        cut = pl.ds(n * CW, CW)
        outs[n] = [pltpu.make_async_copy(gstage.at[turn], grad.at[cut], osem.at[turn]),
                   pltpu.make_async_copy(fstage.at[turn], fish.at[cut], osem.at[2 + turn])]
        for cp in outs[n]:
            cp.start()

    for k in range(1, 4):
        @pl.when(sec > 3 - k)
        def _():
            cin[k - 1] = jnp.zeros_like(cin[k - 1])

    def terms(n):
        for m in range(M):
            if n == NC - 1:
                r2[m, n].wait_recv()
                total = pown[m, n, 0:T] + rin[m, n, 0:T].astype(F32)
            else:
                total = pown[m, n, 0:T]
                for du in range(1, 4):
                    r3[m, n, du].wait_recv()
                    total = total + sin[m, n, du - 1].astype(F32)
            csend[n, m] = total.astype(BF16)
            pown[m, n, 0:T] = total
            for k in range(1, 4):
                @pl.when(sec >= k)
                def _():
                    down[n, k, m].start()

    def sums(n):
        cut = pl.ds(n * CW, CW)
        for m in range(M):
            total = tv[m, :, cut].astype(F32) + pown[m, n, 0:T]
            for k in range(1, 4):
                @pl.when(sec <= 3 - k)
                def _():
                    down[n, k, m].wait_recv()
                total = total + cin[k - 1, n, m].astype(F32)
            rstage[m, :, cut] = total.astype(BF16)

    def gathered_all():
        for m in range(M):
            for zz in range(2):
                for side in range(2):
                    tf[m, zz, side].wait_recv()

    plan = [(combine, 0), (combine, 1), (spread, 0), (combine, 2), (gathered_all,), (send_rows, 0), (terms, 0),
            (spread, 1), (combine, 3), (send_rows, 1), (terms, 1), (spread, 2), (spread, 3), (send_rows, 2),
            (terms, 2), (send_rows, 3), (terms, 3), (weights, 0), (sums, 0), (weights, 1), (sums, 1), (weights, 2),
            (sums, 2), (sums, 3), (weights, 3)]
    for step, *at in plan:
        step(*at)

    out_r = pltpu.make_async_copy(rstage, resid, lsem.at[5])
    out_r.start()
    for cp in started:
        cp.wait_recv()
        cp.wait_send()

    for k in range(1, 4):
        @pl.when(sec >= k)
        def _():
            for n in range(NC):
                for m in range(M):
                    down[n, k, m].wait_send()

    for n in outs:
        if n + 2 not in outs:
            for cp in outs[n]:
                cp.wait()
    out_r.wait()


def fused(act, routes, gates, hcot, wgt, top):
    hbm = pl.BlockSpec(memory_space=pl.ANY)
    vmem = pl.BlockSpec(memory_space=pltpu.VMEM)
    sem = pltpu.SemaphoreType.DMA
    v = pltpu.VMEM
    pairs = [M, M * 7, M * 7, M * 4, M * 4, M * 7, M * NC * 7, M * NC, M * NC * 3, M * NC * 7, M * NC * 3]
    sems = [sem((6,)), sem((4,))]
    for n in pairs:
        sems += [sem((n,)), sem((n,))]
    return pl.pallas_call(
        kernel,
        out_shape=(
            jax.ShapeDtypeStruct((D, F), BF16),
            jax.ShapeDtypeStruct((D, F), BF16),
            jax.ShapeDtypeStruct((M, T, D), BF16),
        ),
        in_specs=[hbm, vmem, vmem, hbm, hbm, hbm],
        out_specs=(hbm, hbm, hbm),
        scratch_shapes=[
            v((M, NB, 16, 128), BF16),
            v((M, NB, T, 128), BF16),
            v((M, NB, T, D), BF16),
            v((M, NI * ROWS, NB * T), BF16),
            v((M, NB * T, NI * ROWS), BF16),
            v((M, 16, 128), BF16),
            v((M, NI, 16, 128), BF16),
            v((F, F), BF16),
            v((M, F, F), BF16),
            v((D, F), BF16),
            v((M, T, D), BF16),
            v((M, NI * ROWS, F), BF16),
            v((M, NC, NI * ROWS, CW), BF16),
            v((M, NC, NI * ROWS, CW), BF16),
            v((M, NC, NI * ROWS, CW), BF16),
            v((M, NC, 4 * T, CW), F32),
            v((M, NC, 4 * T, CW), BF16),
            v((M, NC, 4 * T, CW), BF16),
            v((M, NC - 1, 3, T, CW), BF16),
            v((M, NC - 1, 3, T, CW), BF16),
            v((M, 3, 2, T, CW), BF16),
            v((M, 3, 2, T, CW), BF16),
            v((NC, M, T, CW), BF16),
            v((3, NC, M, T, CW), BF16),
            v((M, T, D), BF16),
            v((2, CW, F), BF16),
            v((2, CW, F), BF16),
        ] + sems,
        compiler_params=pltpu.CompilerParams(
            collective_id=0, has_side_effects=True, vmem_limit_bytes=62 * 2**20),
        cost_estimate=pl.CostEstimate(flops=18 * 10**9, bytes_accessed=26 * 10**6, transcendentals=0),
        name="expert_backward",
    )(act, routes, gates, hcot, wgt, top)


def shards(activations, routes, gates, hidden_cot, weight, top_cot):
    grad, fish, resid = fused(
        activations[0], jnp.swapaxes(routes[0], 1, 2), jnp.swapaxes(gates[0], 1, 2), hidden_cot[0, :, 0], weight[0, 0], top_cot)
    return grad[None, None], fish[None, None], resid[None]


def solution(mesh):
    return jax.shard_map(
        shards,
        mesh=mesh,
        in_specs=(
            P("section", None, "dp", None),
            P("section", None, "dp", None),
            P("section", None, "dp", None),
            P("section", None, "dp", None, None),
            P("section", "dp", None, None),
            P(None, "dp", None),
        ),
        out_specs=(
            P("section", "dp", None, None),
            P("section", "dp", None, None),
            P("section", None, "dp", None),
        ),
        check_vma=False,
    )
```

```python
import jax
import jax.numpy as jnp
from jax import lax
from jax.experimental import pallas as pl
from jax.experimental.pallas import tpu as pltpu
from jax.sharding import PartitionSpec as P

MESH = pl.DeviceIdType.MESH
M = 2
T = 64
D = 2048
F = 768
E = 64
CAP = 12
NB = 8
NI = 8
ROWS = NB * CAP
NC = 4
CW = D // NC
NT = (((1,), (1,)), ((), ()))
TN = (((0,), (0,)), ((), ()))
F32 = jnp.float32
BF16 = jnp.bfloat16


def dot(a, b, dims=(((1,), (0,)), ((), ()))):
    return lax.dot_general(a, b, dims, preferred_element_type=F32)


def iota(shape, dim):
    return lax.broadcasted_iota(jnp.int32, shape, dim)


class Copy:
    def __init__(self, copy, started):
        self.copy, self.started = copy, started
        self.sent = self.received = False

    def start(self):
        self.copy.start()
        self.started.append(self)

    def wait_recv(self):
        if not self.received:
            self.copy.wait_recv()
        self.received = True

    def wait_send(self):
        if not self.sent:
            self.copy.wait_send()
        self.sent = True


def kernel(
    act, routes, gates, hcot, wgt, top,
    grad, fish, resid,
    slot, meta, tok, hh, hht, gsend, gin, pick, hc, wv, tv, scaled, bsend, bin_, rows,
    pown, psend, rin, ssend, sin, lsend, lin, csend, cin, xin, rstage, gstage, fstage,
    lsem, osem, tz_s, tz_r, su_s, su_r, mu_s, mu_r, tu_s, tu_r, tf_s, tf_r, g_s, g_r,
    r1_s, r1_r, r2_s, r2_r, r3_s, r3_r, d3_s, d3_r, ch_s, ch_r, x_s, x_r,
):
    sec = lax.axis_index("section")
    me = lax.axis_index("dp")
    y, x, z, c = me // 16, (me // 4) % 4, (me // 2) % 2, me % 2

    def index(yy, xx, zz, cc):
        return ((yy * 4 + xx) * 2 + zz) * 2 + cc

    def peer_u(m, du, dz=0):
        if m == 0:
            return index((y + du) % 4, x, (z + dz) % 2, c)
        return index(y, (x + du) % 4, (z + dz) % 2, c)

    def peer_v(m, dv, dc):
        if m == 0:
            return index(y, (x + dv) % 4, z, (c + dc) % 2)
        return index((y + dv) % 4, x, z, (c + dc) % 2)

    peer_z = index(y, x, 1 - z, c)

    started = []

    def remote(src, dst, ssem, rsem, dev):
        return Copy(pltpu.make_async_remote_copy(
            src_ref=src, dst_ref=dst, send_sem=ssem, recv_sem=rsem,
            device_id={"dp": dev}, device_id_type=MESH), started)

    act_cp = [pltpu.make_async_copy(act.at[m], tok.at[m, 0], lsem.at[m]) for m in range(M)]
    hc_cp = pltpu.make_async_copy(hcot, hc, lsem.at[2])
    w_cp = pltpu.make_async_copy(wgt, wv, lsem.at[3])
    t_cp = pltpu.make_async_copy(top, tv, lsem.at[4])
    for cp in act_cp + [hc_cp, w_cp, t_cp]:
        cp.start()

    bar = pltpu.get_barrier_semaphore()
    peers = [peer_z, index(y, x, z, 1 - c)]
    for du in range(1, 4):
        peers += [index((y + du) % 4, x, 1 - z, c), index(y, (x + du) % 4, 1 - z, c)]
    for m in range(M):
        for dv in range(1, 4):
            for dc in range(2):
                peers.append(peer_v(m, dv, dc))
    for p in peers:
        pl.semaphore_signal(bar, inc=1, device_id={"dp": p}, device_id_type=MESH)
    for ds in (1, 2, 3):
        pl.semaphore_signal(bar, inc=1, device_id={"section": (sec + ds) % 4}, device_id_type=MESH)

    expert = iota((128, T), 0) & (E - 1)
    lower = (iota((T, T), 0) > iota((T, T), 1)).astype(F32).astype(BF16)
    same = (iota((T, T), 0) == iota((T, T), 1)).astype(F32).astype(BF16)
    for m in range(M):
        r = routes[m]
        g = gates[m].astype(F32)
        named = jnp.zeros((128, T), F32)
        gate = jnp.zeros((128, T), F32)
        for k in range(8):
            eq = r[k:k + 1] == expert
            named = jnp.where(eq, 1.0, named)
            gate = jnp.where(eq, g[k:k + 1], gate)
        named = named.astype(BF16)
        pos = jnp.where(dot(same, named, NT) > 0.0, dot(lower, named, NT), 128.0)
        gate = dot(same, gate.astype(BF16), NT)
        meta[m, 0] = pos.astype(BF16)
        slots = [jnp.sum(jnp.where(pos == float(q), gate, 0.0), axis=0, keepdims=True) for q in range(CAP)]
        slots.append(jnp.zeros((16 - CAP, 128), F32))
        slot[m, 0] = jnp.concatenate(slots, axis=0).astype(BF16)

    pl.semaphore_wait(bar, len(peers) + 3)

    tz = [remote(tok.at[m, 0], tok.at[m, 4], tz_s.at[m], tz_r.at[m], peer_z) for m in range(M)]
    mu = {}
    su = {}
    tu = {}
    tf = {}
    for m in range(M):
        for zz in range(2):
            at = zz * 4
            for du in range(4):
                if zz or du:
                    k = m * 7 + zz * 4 + du - 1
                    su[m, zz, du] = remote(slot.at[m, 0], slot.at[m, at + (4 - du) % 4], su_s.at[k], su_r.at[k],
                                           peer_u(m, du, zz))
                    mu[m, zz, du] = remote(meta.at[m, 0], meta.at[m, at + (4 - du) % 4], mu_s.at[k], mu_r.at[k],
                                           peer_u(m, du, zz))
            for side, du in enumerate((1, 3)):
                k = (m * 2 + zz) * 2 + side
                half = pl.ds(side * (T // 2), T // 2)
                tu[m, zz, side] = remote(tok.at[m, at], tok.at[m, at + 4 - du], tu_s.at[k], tu_r.at[k], peer_u(m, du))
                tf[m, zz, side] = remote(tok.at[m, at + 4 - du, half], tok.at[m, at + 2, half],
                                         tf_s.at[k], tf_r.at[k], peer_u(m, du))

    def forward(zz):
        for m in range(M):
            for side in range(2):
                tu[m, zz, side].wait_recv()
                tf[m, zz, side].start()

    for at in su:
        su[at].start()
    for m in range(M):
        act_cp[m].wait()
        for side in range(2):
            tu[m, 0, side].start()
        tz[m].start()
    for at in su:
        su[at].wait_recv()

    def exchange_expert(m, i):
        dv, dc = i >> 1, i & 1
        if m == 0:
            return index(y, (x + dv) & 3, z, (c + dc) & 1)
        return index((y + dv) & 3, x, z, (c + dc) & 1)

    gcopy = {}
    for m in range(M):
        table = slot[m].reshape(NB * 16, 128)
        sel = (iota((16, 128), 1) == exchange_expert(m, iota((16, 128), 0) & 7)).astype(F32).astype(BF16)
        gsend[m] = dot(sel, table, NT).astype(BF16)
        for i in range(1, NI):
            k = m * 7 + i - 1
            gcopy[m, i] = remote(gsend.at[m], gin.at[m, i], g_s.at[k], g_r.at[k], peer_v(m, i // 2, i % 2))
            gcopy[m, i].start()

    def row_masks(m):
        block = meta[m].reshape(NB * T, 128)
        r = iota((NI * ROWS, 128), 0)
        i = (r * 683) >> 16
        sel = (iota((NI * ROWS, 128), 1) == exchange_expert(m, i)).astype(F32).astype(BF16)
        r = iota((NI * ROWS, NB * T), 0)
        want = r - ((r * 683) >> 16) * ROWS - CAP * (iota((NI * ROWS, NB * T), 1) >> 6)
        hh[m] = (dot(sel, block, NT) == want.astype(F32)).astype(F32).astype(BF16)

    for at in mu:
        mu[at].start()
    forward(0)
    for m in range(M):
        tz[m].wait_recv()
        for side in range(2):
            tu[m, 1, side].start()

    hc_cp.wait()
    r = iota((ROWS, 128), 0)
    b = (r * 171) >> 11
    place = (iota((ROWS, 128), 1) == b * 16 + r - b * CAP).astype(F32).astype(BF16)
    r = iota((ROWS, 1), 0)
    b = (r * 171) >> 11
    q = r - b * CAP
    zs = (z + (b >> 2)) & 1
    us = b & 3
    for m in range(M):
        for i in range(1, NI):
            gcopy[m, i].wait_recv()
        for i in range(NI):
            dv, dc = i // 2, i % 2
            got = gsend[m] if i == 0 else gin[m, i]
            gcol = dot(place, got, NT)[:, i:i + 1]
            if m == 0:
                j = index((y + us) & 3, (x + 4 - dv) % 4, zs, (c + dc) % 2)
            else:
                j = index((y + 4 - dv) % 4, (x + us) & 3, zs, (c + dc) % 2)
            pick[i * ROWS:(i + 1) * ROWS] = jnp.where(iota((ROWS, F), 1) == j * CAP + q, gcol, 0.0).astype(BF16)
        scaled[m] = dot(pick[...], hc[m]).astype(BF16)

    w_cp.wait()
    r1 = {}
    d3 = {}
    for n in range(NC):
        for m in range(M):
            for i in range(1, NI):
                dv, dc = i // 2, i % 2
                k = (m * NC + n) * 7 + i - 1
                part = pl.ds(i * ROWS, ROWS)
                r1[m, n, i] = remote(bsend.at[m, n, part], bin_.at[m, n, part], r1_s.at[k], r1_r.at[k],
                                     peer_v(m, (4 - dv) % 4, dc))
                d3[m, n, i] = remote(bsend.at[m, n, part], rows.at[m, n, part], d3_s.at[k], d3_r.at[k],
                                     peer_v(m, dv, dc))
    for n in range(NC):
        for m in range(M):
            back = dot(scaled[m], wv[n * CW:(n + 1) * CW], NT).astype(BF16)
            bin_[m, n, 0:ROWS] = back[0:ROWS]
            bsend[m, n, ROWS:] = back[ROWS:]
            for i in range(1, NI):
                r1[m, n, i].start()

    forward(1)
    for at in mu:
        mu[at].wait_recv()
    for m in range(M):
        block = meta[m].reshape(NB * T, 128)
        l = iota((128, NI * ROWS), 1)
        i = (l * 683) >> 16
        sel = (iota((128, NI * ROWS), 0) == exchange_expert(m, i)).astype(F32).astype(BF16)
        l = iota((NB * T, NI * ROWS), 1)
        want = l - ((l * 683) >> 16) * ROWS - CAP * (iota((NB * T, NI * ROWS), 0) >> 6)
        hht[m] = (dot(block, sel) == want.astype(F32)).astype(F32).astype(BF16)

    for m in range(M):
        row_masks(m)
    t_cp.wait()

    r2 = {}
    r3 = {}
    for m in range(M):
        n = NC - 1
        near = pl.ds(0, T)
        r2[m, n] = remote(psend.at[m, n, near], rin.at[m, n, near], r2_s.at[m * NC + n], r2_r.at[m * NC + n], peer_z)
        for du in range(1, 4):
            k = (m * NC + n) * 3 + du - 1
            r3[m, n, du] = remote(lsend.at[m, du - 1], lin.at[m, du - 1], r3_s.at[k], r3_r.at[k], peer_u(m, du))
    for n in range(NC - 1):
        for m in range(M):
            k = m * NC + n
            r2[m, n] = remote(psend.at[m, n], rin.at[m, n], r2_s.at[k], r2_r.at[k], peer_z)
            for du in range(1, 4):
                k = (m * NC + n) * 3 + du - 1
                r3[m, n, du] = remote(ssend.at[m, n, du - 1], sin.at[m, n, du - 1], r3_s.at[k], r3_r.at[k],
                                      peer_u(m, du))
    ch = {(n, m): pltpu.make_async_remote_copy(
        src_ref=csend.at[n, m], dst_ref=cin.at[n, m], send_sem=ch_s.at[n * M + m], recv_sem=ch_r.at[n * M + m],
        device_id={"section": (sec + 3) % 4}, device_id_type=MESH) for n in range(NC - 1) for m in range(M)}
    last = {(k, m): pltpu.make_async_remote_copy(
        src_ref=csend.at[NC - 1, m], dst_ref=xin.at[k - 1, m],
        send_sem=x_s.at[(k - 1) * M + m], recv_sem=x_r.at[(k - 1) * M + m],
        device_id={"section": (sec + 4 - k) % 4}, device_id_type=MESH) for k in range(1, 4) for m in range(M)}

    def combine(n):
        for m in range(M):
            for i in range(1, NI):
                r1[m, n, i].wait_recv()
            part = dot(hht[m], bin_[m, n])
            if n == NC - 1:
                for zz in range(2):
                    for du in range(4):
                        one = part[(zz * 4 + du) * T:(zz * 4 + du + 1) * T]
                        if du == 0:
                            pown[m, n, zz * T:(zz + 1) * T] = one
                        else:
                            lsend[m, du - 1, zz] = one.astype(BF16)
                for du in range(1, 4):
                    r3[m, n, du].start()
                continue
            psend[m, n] = part[4 * T:].astype(BF16)
            r2[m, n].start()
            pown[m, n] = part[:4 * T]

    def send_rows(n):
        for m in range(M):
            for i in range(1, NI):
                r1[m, n, i].wait_send()
            gathered = tok[m, :, :, n * CW:(n + 1) * CW].reshape(NB * T, CW)
            out = dot(hh[m], gathered).astype(BF16)
            rows[m, n, 0:ROWS] = out[0:ROWS]
            bsend[m, n, ROWS:] = out[ROWS:]
            for i in range(1, NI):
                d3[m, n, i].start()

    def spread(n):
        for m in range(M):
            if n == NC - 1:
                total = [pown[m, n, zz * T:(zz + 1) * T] for zz in range(2)]
                for du in range(1, 4):
                    r3[m, n, du].wait_recv()
                    total = [total[zz] + lin[m, du - 1, zz].astype(F32) for zz in range(2)]
                psend[m, n, 0:T] = total[1].astype(BF16)
                r2[m, n].start()
                pown[m, n, 0:T] = total[0]
                continue
            r2[m, n].wait_recv()
            total = pown[m, n] + rin[m, n].astype(F32)
            for du in range(1, 4):
                ssend[m, n, du - 1] = total[du * T:(du + 1) * T].astype(BF16)
                r3[m, n, du].start()
            pown[m, n, 0:T] = total[0:T]

    outs = {}

    def weights(n):
        turn = n % 2
        if n >= 2:
            for cp in outs[n - 2]:
                cp.wait()
        for m in range(M):
            for i in range(1, NI):
                d3[m, n, i].wait_recv()
        p0 = dot(rows[0, n], scaled[0], TN)
        p1 = dot(rows[1, n], scaled[1], TN)
        gstage[turn] = (p0 + p1).astype(BF16)
        fstage[turn] = (p0 * p0 + p1 * p1).astype(BF16)
        cut = pl.ds(n * CW, CW)
        outs[n] = [pltpu.make_async_copy(gstage.at[turn], grad.at[cut], osem.at[turn]),
                   pltpu.make_async_copy(fstage.at[turn], fish.at[cut], osem.at[2 + turn])]
        for cp in outs[n]:
            cp.start()

    @pl.when(sec == 3)
    def _():
        cin[...] = jnp.zeros_like(cin)

    for k in range(1, 4):
        @pl.when(sec > 3 - k)
        def _():
            xin[k - 1] = jnp.zeros_like(xin[k - 1])

    def chain(n):
        for m in range(M):
            for du in range(1, 4):
                r3[m, n, du].copy.wait_recv()
                r3[m, n, du].received = True

            @pl.when(sec < 3)
            def _():
                ch[n, m].wait_recv()

            total = pown[m, n, 0:T] + cin[n, m].astype(F32)
            for du in range(1, 4):
                total = total + sin[m, n, du - 1].astype(F32)
            csend[n, m] = total.astype(BF16)

            @pl.when(sec > 0)
            def _():
                ch[n, m].start()

            cut = pl.ds(n * CW, CW)
            rstage[m, :, cut] = (tv[m, :, cut].astype(F32) + total).astype(BF16)

    def chain_on(section, n):
        @pl.when(sec == section)
        def _():
            chain(n)

    def last_terms():
        n = NC - 1
        for m in range(M):
            r2[m, n].wait_recv()
            total = pown[m, n, 0:T] + rin[m, n, 0:T].astype(F32)
            csend[n, m] = total.astype(BF16)
            pown[m, n, 0:T] = total
            for k in range(1, 4):
                @pl.when(sec >= k)
                def _():
                    last[k, m].start()

    def last_sums():
        n = NC - 1
        cut = pl.ds(n * CW, CW)
        for m in range(M):
            total = tv[m, :, cut].astype(F32) + pown[m, n, 0:T]
            for k in range(1, 4):
                @pl.when(sec <= 3 - k)
                def _():
                    last[k, m].wait_recv()
                total = total + xin[k - 1, m].astype(F32)
            rstage[m, :, cut] = total.astype(BF16)

    def gathered_all():
        for m in range(M):
            for zz in range(2):
                for side in range(2):
                    tf[m, zz, side].wait_recv()

    plan = [(combine, 0), (combine, 1), (spread, 0), (combine, 2), (gathered_all,), (send_rows, 0), (chain_on, 3, 0),
            (spread, 1), (combine, 3), (send_rows, 1), (chain_on, 3, 1), (chain_on, 2, 0), (spread, 2), (spread, 3),
            (send_rows, 2), (chain_on, 3, 2), (chain_on, 2, 1), (chain_on, 1, 0), (send_rows, 3), (last_terms,),
            (chain_on, 0, 0), (chain_on, 1, 1), (chain_on, 2, 2), (weights, 0), (chain_on, 0, 1), (weights, 1),
            (chain_on, 1, 2), (weights, 2), (chain_on, 0, 2), (last_sums,), (weights, 3)]
    for step, *at in plan:
        step(*at)

    out_r = pltpu.make_async_copy(rstage, resid, lsem.at[5])
    out_r.start()
    for cp in started:
        cp.wait_recv()
        cp.wait_send()

    @pl.when(sec > 0)
    def _():
        for at in ch:
            ch[at].wait_send()

    for k in range(1, 4):
        @pl.when(sec >= k)
        def _():
            for m in range(M):
                last[k, m].wait_send()

    for n in outs:
        if n + 2 not in outs:
            for cp in outs[n]:
                cp.wait()
    out_r.wait()


def fused(act, routes, gates, hcot, wgt, top):
    hbm = pl.BlockSpec(memory_space=pl.ANY)
    vmem = pl.BlockSpec(memory_space=pltpu.VMEM)
    sem = pltpu.SemaphoreType.DMA
    v = pltpu.VMEM
    pairs = [M, M * 7, M * 7, M * 4, M * 4, M * 7, M * NC * 7, M * NC, M * NC * 3, M * NC * 7, M * (NC - 1), M * 3]
    sems = [sem((6,)), sem((4,))]
    for n in pairs:
        sems += [sem((n,)), sem((n,))]
    return pl.pallas_call(
        kernel,
        out_shape=(
            jax.ShapeDtypeStruct((D, F), BF16),
            jax.ShapeDtypeStruct((D, F), BF16),
            jax.ShapeDtypeStruct((M, T, D), BF16),
        ),
        in_specs=[hbm, vmem, vmem, hbm, hbm, hbm],
        out_specs=(hbm, hbm, hbm),
        scratch_shapes=[
            v((M, NB, 16, 128), BF16),
            v((M, NB, T, 128), BF16),
            v((M, NB, T, D), BF16),
            v((M, NI * ROWS, NB * T), BF16),
            v((M, NB * T, NI * ROWS), BF16),
            v((M, 16, 128), BF16),
            v((M, NI, 16, 128), BF16),
            v((F, F), BF16),
            v((M, F, F), BF16),
            v((D, F), BF16),
            v((M, T, D), BF16),
            v((M, NI * ROWS, F), BF16),
            v((M, NC, NI * ROWS, CW), BF16),
            v((M, NC, NI * ROWS, CW), BF16),
            v((M, NC, NI * ROWS, CW), BF16),
            v((M, NC, 4 * T, CW), F32),
            v((M, NC, 4 * T, CW), BF16),
            v((M, NC, 4 * T, CW), BF16),
            v((M, NC - 1, 3, T, CW), BF16),
            v((M, NC - 1, 3, T, CW), BF16),
            v((M, 3, 2, T, CW), BF16),
            v((M, 3, 2, T, CW), BF16),
            v((NC, M, T, CW), BF16),
            v((NC - 1, M, T, CW), BF16),
            v((3, M, T, CW), BF16),
            v((M, T, D), BF16),
            v((2, CW, F), BF16),
            v((2, CW, F), BF16),
        ] + sems,
        compiler_params=pltpu.CompilerParams(
            collective_id=0, has_side_effects=True, vmem_limit_bytes=62 * 2**20),
        cost_estimate=pl.CostEstimate(flops=18 * 10**9, bytes_accessed=26 * 10**6, transcendentals=0),
        name="expert_backward",
    )(act, routes, gates, hcot, wgt, top)


def hand_on(grad, fish, resid, grad_out, fish_out, resid_out, gbuf, fbuf, rbuf, in_sems, out_sems):
    cuts = [pl.ds(n * CW, CW) for n in range(NC)]
    ways = []
    for cut in cuts:
        ways.append((grad.at[cut], gbuf.at[cut], grad_out.at[cut]))
        ways.append((fish.at[cut], fbuf.at[cut], fish_out.at[cut]))
    ways.append((resid, rbuf, resid_out))
    loads = [pltpu.make_async_copy(a, b, in_sems.at[k]) for k, (a, b, _) in enumerate(ways)]
    stores = [pltpu.make_async_copy(b, c, out_sems.at[k]) for k, (_, b, c) in enumerate(ways)]
    for cp in loads:
        cp.start()
    for load, store in zip(loads, stores):
        load.wait()
        store.start()
    for cp in stores:
        cp.wait()


def handed_on(*arrays):
    hbm = pl.BlockSpec(memory_space=pl.ANY)
    return pl.pallas_call(
        hand_on,
        out_shape=tuple(jax.ShapeDtypeStruct(a.shape, a.dtype) for a in arrays),
        in_specs=[hbm] * 3,
        out_specs=(hbm,) * 3,
        scratch_shapes=[pltpu.VMEM(a.shape, a.dtype) for a in arrays]
        + [pltpu.SemaphoreType.DMA((2 * NC + 1,))] * 2,
        compiler_params=pltpu.CompilerParams(vmem_limit_bytes=60 * 2**20),
        name="results",
    )(*arrays)


def shards(activations, routes, gates, hidden_cot, weight, top_cot):
    grad, fish, resid = fused(
        activations[0], jnp.swapaxes(routes[0], 1, 2), jnp.swapaxes(gates[0], 1, 2), hidden_cot[0, :, 0], weight[0, 0], top_cot)
    grad, fish, resid = handed_on(grad, fish, resid)
    return grad[None, None], fish[None, None], resid[None]


def solution(mesh):
    return jax.shard_map(
        shards,
        mesh=mesh,
        in_specs=(
            P("section", None, "dp", None),
            P("section", None, "dp", None),
            P("section", None, "dp", None),
            P("section", None, "dp", None, None),
            P("section", "dp", None, None),
            P(None, "dp", None),
        ),
        out_specs=(
            P("section", "dp", None, None),
            P("section", "dp", None, None),
            P("section", None, "dp", None),
        ),
        check_vma=False,
    )
```

```python
import jax
import jax.numpy as jnp
from jax import lax
from jax.experimental import pallas as pl
from jax.experimental.pallas import tpu as pltpu
from jax.sharding import PartitionSpec as P

MESH = pl.DeviceIdType.MESH
M = 2
T = 64
D = 2048
F = 768
E = 64
CAP = 12
NB = 8
NI = 8
ROWS = NB * CAP
NC = 4
CW = D // NC
NT = (((1,), (1,)), ((), ()))
TN = (((0,), (0,)), ((), ()))
F32 = jnp.float32
BF16 = jnp.bfloat16


def dot(a, b, dims=(((1,), (0,)), ((), ()))):
    return lax.dot_general(a, b, dims, preferred_element_type=F32)


def iota(shape, dim):
    return lax.broadcasted_iota(jnp.int32, shape, dim)


class Copy:
    def __init__(self, copy, started):
        self.copy, self.started = copy, started
        self.sent = self.received = False

    def start(self):
        self.copy.start()
        self.started.append(self)

    def wait_recv(self):
        if not self.received:
            self.copy.wait_recv()
        self.received = True

    def wait_send(self):
        if not self.sent:
            self.copy.wait_send()
        self.sent = True


def kernel(
    act, routes, gates, hcot, wgt, top,
    grad, fish, resid,
    slot, meta, tok, hh, hht, gsend, gin, pick, hc, wv, tv, scaled, bsend, bin_, rows,
    pown, psend, rin, ssend, sin, lsend, lin, csend, cin, xin, rstage, gstage, fstage,
    lsem, osem, tz_s, tz_r, su_s, su_r, mu_s, mu_r, tu_s, tu_r, tf_s, tf_r, g_s, g_r,
    r1_s, r1_r, r2_s, r2_r, r3_s, r3_r, d3_s, d3_r, ch_s, ch_r, x_s, x_r,
):
    sec = lax.axis_index("section")
    me = lax.axis_index("dp")
    y, x, z, c = me // 16, (me // 4) % 4, (me // 2) % 2, me % 2

    def index(yy, xx, zz, cc):
        return ((yy * 4 + xx) * 2 + zz) * 2 + cc

    def peer_u(m, du, dz=0):
        if m == 0:
            return index((y + du) % 4, x, (z + dz) % 2, c)
        return index(y, (x + du) % 4, (z + dz) % 2, c)

    def peer_v(m, dv, dc):
        if m == 0:
            return index(y, (x + dv) % 4, z, (c + dc) % 2)
        return index((y + dv) % 4, x, z, (c + dc) % 2)

    peer_z = index(y, x, 1 - z, c)

    started = []

    def remote(src, dst, ssem, rsem, dev):
        return Copy(pltpu.make_async_remote_copy(
            src_ref=src, dst_ref=dst, send_sem=ssem, recv_sem=rsem,
            device_id={"dp": dev}, device_id_type=MESH), started)

    act_cp = [pltpu.make_async_copy(act.at[m], tok.at[m, 0], lsem.at[m]) for m in range(M)]
    hc_cp = pltpu.make_async_copy(hcot, hc, lsem.at[2])
    w_cp = pltpu.make_async_copy(wgt, wv, lsem.at[3])
    t_cp = pltpu.make_async_copy(top, tv, lsem.at[4])
    for cp in act_cp + [hc_cp, w_cp, t_cp]:
        cp.start()

    bar = pltpu.get_barrier_semaphore()
    peers = [peer_z, index(y, x, z, 1 - c)]
    for du in range(1, 4):
        peers += [index((y + du) % 4, x, 1 - z, c), index(y, (x + du) % 4, 1 - z, c)]
    for m in range(M):
        for dv in range(1, 4):
            for dc in range(2):
                peers.append(peer_v(m, dv, dc))
    for p in peers:
        pl.semaphore_signal(bar, inc=1, device_id={"dp": p}, device_id_type=MESH)
    for ds in (1, 2, 3):
        pl.semaphore_signal(bar, inc=1, device_id={"section": (sec + ds) % 4}, device_id_type=MESH)

    expert = iota((128, T), 0) & (E - 1)
    lower = (iota((T, T), 0) > iota((T, T), 1)).astype(F32).astype(BF16)
    same = (iota((T, T), 0) == iota((T, T), 1)).astype(F32).astype(BF16)
    for m in range(M):
        r = routes[m]
        g = gates[m].astype(F32)
        named = jnp.zeros((128, T), F32)
        gate = jnp.zeros((128, T), F32)
        for k in range(8):
            eq = r[k:k + 1] == expert
            named = jnp.where(eq, 1.0, named)
            gate = jnp.where(eq, g[k:k + 1], gate)
        named = named.astype(BF16)
        pos = jnp.where(dot(same, named, NT) > 0.0, dot(lower, named, NT), 128.0)
        gate = dot(same, gate.astype(BF16), NT)
        meta[m, 0] = pos.astype(BF16)
        slots = [jnp.sum(jnp.where(pos == float(q), gate, 0.0), axis=0, keepdims=True) for q in range(CAP)]
        slots.append(jnp.zeros((16 - CAP, 128), F32))
        slot[m, 0] = jnp.concatenate(slots, axis=0).astype(BF16)

    pl.semaphore_wait(bar, len(peers) + 3)

    tz = [remote(tok.at[m, 0], tok.at[m, 4], tz_s.at[m], tz_r.at[m], peer_z) for m in range(M)]
    mu = {}
    su = {}
    tu = {}
    tf = {}
    for m in range(M):
        for zz in range(2):
            at = zz * 4
            for du in range(4):
                if zz or du:
                    k = m * 7 + zz * 4 + du - 1
                    su[m, zz, du] = remote(slot.at[m, 0], slot.at[m, at + (4 - du) % 4], su_s.at[k], su_r.at[k],
                                           peer_u(m, du, zz))
                    mu[m, zz, du] = remote(meta.at[m, 0], meta.at[m, at + (4 - du) % 4], mu_s.at[k], mu_r.at[k],
                                           peer_u(m, du, zz))
            for side, du in enumerate((1, 3)):
                k = (m * 2 + zz) * 2 + side
                half = pl.ds(side * (T // 2), T // 2)
                tu[m, zz, side] = remote(tok.at[m, at], tok.at[m, at + 4 - du], tu_s.at[k], tu_r.at[k], peer_u(m, du))
                tf[m, zz, side] = remote(tok.at[m, at + 4 - du, half], tok.at[m, at + 2, half],
                                         tf_s.at[k], tf_r.at[k], peer_u(m, du))

    def forward(zz):
        for m in range(M):
            for side in range(2):
                tu[m, zz, side].wait_recv()
                tf[m, zz, side].start()

    for at in su:
        su[at].start()
    for m in range(M):
        act_cp[m].wait()
        for side in range(2):
            tu[m, 0, side].start()
        tz[m].start()
    for at in su:
        su[at].wait_recv()

    def exchange_expert(m, i):
        dv, dc = i >> 1, i & 1
        if m == 0:
            return index(y, (x + dv) & 3, z, (c + dc) & 1)
        return index((y + dv) & 3, x, z, (c + dc) & 1)

    gcopy = {}
    for m in range(M):
        table = slot[m].reshape(NB * 16, 128)
        sel = (iota((16, 128), 1) == exchange_expert(m, iota((16, 128), 0) & 7)).astype(F32).astype(BF16)
        gsend[m] = dot(sel, table, NT).astype(BF16)
        for i in range(1, NI):
            k = m * 7 + i - 1
            gcopy[m, i] = remote(gsend.at[m], gin.at[m, i], g_s.at[k], g_r.at[k], peer_v(m, i // 2, i % 2))
            gcopy[m, i].start()

    def row_masks(m):
        block = meta[m].reshape(NB * T, 128)
        r = iota((NI * ROWS, 128), 0)
        i = (r * 683) >> 16
        sel = (iota((NI * ROWS, 128), 1) == exchange_expert(m, i)).astype(F32).astype(BF16)
        r = iota((NI * ROWS, NB * T), 0)
        want = r - ((r * 683) >> 16) * ROWS - CAP * (iota((NI * ROWS, NB * T), 1) >> 6)
        hh[m] = (dot(sel, block, NT) == want.astype(F32)).astype(F32).astype(BF16)

    for at in mu:
        mu[at].start()
    forward(0)

    hc_cp.wait()
    r = iota((ROWS, 128), 0)
    b = (r * 171) >> 11
    place = (iota((ROWS, 128), 1) == b * 16 + r - b * CAP).astype(F32).astype(BF16)
    r = iota((ROWS, 1), 0)
    b = (r * 171) >> 11
    q = r - b * CAP
    zs = (z + (b >> 2)) & 1
    us = b & 3
    for m in range(M):
        for i in range(1, NI):
            gcopy[m, i].wait_recv()
        for i in range(NI):
            dv, dc = i // 2, i % 2
            got = gsend[m] if i == 0 else gin[m, i]
            gcol = dot(place, got, NT)[:, i:i + 1]
            if m == 0:
                j = index((y + us) & 3, (x + 4 - dv) % 4, zs, (c + dc) % 2)
            else:
                j = index((y + 4 - dv) % 4, (x + us) & 3, zs, (c + dc) % 2)
            pick[i * ROWS:(i + 1) * ROWS] = jnp.where(iota((ROWS, F), 1) == j * CAP + q, gcol, 0.0).astype(BF16)
        scaled[m] = dot(pick[...], hc[m]).astype(BF16)

    for m in range(M):
        tz[m].wait_recv()
        for side in range(2):
            tu[m, 1, side].start()

    w_cp.wait()
    r1 = {}
    d3 = {}
    for n in range(NC):
        for m in range(M):
            for i in range(1, NI):
                dv, dc = i // 2, i % 2
                k = (m * NC + n) * 7 + i - 1
                part = pl.ds(i * ROWS, ROWS)
                r1[m, n, i] = remote(bsend.at[m, n, part], bin_.at[m, n, part], r1_s.at[k], r1_r.at[k],
                                     peer_v(m, (4 - dv) % 4, dc))
                d3[m, n, i] = remote(bsend.at[m, n, part], rows.at[m, n, part], d3_s.at[k], d3_r.at[k],
                                     peer_v(m, dv, dc))
    for n in range(NC):
        for m in range(M):
            back = dot(scaled[m], wv[n * CW:(n + 1) * CW], NT).astype(BF16)
            bin_[m, n, 0:ROWS] = back[0:ROWS]
            bsend[m, n, ROWS:] = back[ROWS:]
            for i in range(1, NI):
                r1[m, n, i].start()

    forward(1)
    for at in mu:
        mu[at].wait_recv()
    for m in range(M):
        block = meta[m].reshape(NB * T, 128)
        l = iota((128, NI * ROWS), 1)
        i = (l * 683) >> 16
        sel = (iota((128, NI * ROWS), 0) == exchange_expert(m, i)).astype(F32).astype(BF16)
        l = iota((NB * T, NI * ROWS), 1)
        want = l - ((l * 683) >> 16) * ROWS - CAP * (iota((NB * T, NI * ROWS), 0) >> 6)
        hht[m] = (dot(block, sel) == want.astype(F32)).astype(F32).astype(BF16)

    for m in range(M):
        row_masks(m)
    t_cp.wait()

    r2 = {}
    r3 = {}
    for m in range(M):
        n = NC - 1
        near = pl.ds(0, T)
        r2[m, n] = remote(psend.at[m, n, near], rin.at[m, n, near], r2_s.at[m * NC + n], r2_r.at[m * NC + n], peer_z)
        for du in range(1, 4):
            k = (m * NC + n) * 3 + du - 1
            r3[m, n, du] = remote(lsend.at[m, du - 1], lin.at[m, du - 1], r3_s.at[k], r3_r.at[k], peer_u(m, du))
    for n in range(NC - 1):
        for m in range(M):
            k = m * NC + n
            r2[m, n] = remote(psend.at[m, n], rin.at[m, n], r2_s.at[k], r2_r.at[k], peer_z)
            for du in range(1, 4):
                k = (m * NC + n) * 3 + du - 1
                r3[m, n, du] = remote(ssend.at[m, n, du - 1], sin.at[m, n, du - 1], r3_s.at[k], r3_r.at[k],
                                      peer_u(m, du))
    ch = {(n, m): pltpu.make_async_remote_copy(
        src_ref=csend.at[n, m], dst_ref=cin.at[n, m], send_sem=ch_s.at[n * M + m], recv_sem=ch_r.at[n * M + m],
        device_id={"section": (sec + 3) % 4}, device_id_type=MESH) for n in range(NC - 1) for m in range(M)}
    last = {(k, m): pltpu.make_async_remote_copy(
        src_ref=csend.at[NC - 1, m], dst_ref=xin.at[k - 1, m],
        send_sem=x_s.at[(k - 1) * M + m], recv_sem=x_r.at[(k - 1) * M + m],
        device_id={"section": (sec + 4 - k) % 4}, device_id_type=MESH) for k in range(1, 4) for m in range(M)}

    def combine(n):
        for m in range(M):
            for i in range(1, NI):
                r1[m, n, i].wait_recv()
            part = dot(hht[m], bin_[m, n])
            if n == NC - 1:
                for zz in range(2):
                    for du in range(4):
                        one = part[(zz * 4 + du) * T:(zz * 4 + du + 1) * T]
                        if du == 0:
                            pown[m, n, zz * T:(zz + 1) * T] = one
                        else:
                            lsend[m, du - 1, zz] = one.astype(BF16)
                for du in range(1, 4):
                    r3[m, n, du].start()
                continue
            psend[m, n] = part[4 * T:].astype(BF16)
            r2[m, n].start()
            pown[m, n] = part[:4 * T]

    def send_rows(n):
        for m in range(M):
            for i in range(1, NI):
                r1[m, n, i].wait_send()
            gathered = tok[m, :, :, n * CW:(n + 1) * CW].reshape(NB * T, CW)
            out = dot(hh[m], gathered).astype(BF16)
            rows[m, n, 0:ROWS] = out[0:ROWS]
            bsend[m, n, ROWS:] = out[ROWS:]
            for i in range(1, NI):
                d3[m, n, i].start()

    def spread(n):
        for m in range(M):
            if n == NC - 1:
                total = [pown[m, n, zz * T:(zz + 1) * T] for zz in range(2)]
                for du in range(1, 4):
                    r3[m, n, du].wait_recv()
                    total = [total[zz] + lin[m, du - 1, zz].astype(F32) for zz in range(2)]
                psend[m, n, 0:T] = total[1].astype(BF16)
                r2[m, n].start()
                pown[m, n, 0:T] = total[0]
                continue
            r2[m, n].wait_recv()
            total = pown[m, n] + rin[m, n].astype(F32)
            for du in range(1, 4):
                ssend[m, n, du - 1] = total[du * T:(du + 1) * T].astype(BF16)
                r3[m, n, du].start()
            pown[m, n, 0:T] = total[0:T]

    outs = {}

    def weights(n):
        turn = n % 2
        if n >= 2:
            for cp in outs[n - 2]:
                cp.wait()
        for m in range(M):
            for i in range(1, NI):
                d3[m, n, i].wait_recv()
        p0 = dot(rows[0, n], scaled[0], TN)
        p1 = dot(rows[1, n], scaled[1], TN)
        gstage[turn] = (p0 + p1).astype(BF16)
        fstage[turn] = (p0 * p0 + p1 * p1).astype(BF16)
        cut = pl.ds(n * CW, CW)
        outs[n] = [pltpu.make_async_copy(gstage.at[turn], grad.at[cut], osem.at[turn]),
                   pltpu.make_async_copy(fstage.at[turn], fish.at[cut], osem.at[2 + turn])]
        for cp in outs[n]:
            cp.start()

    @pl.when(sec == 3)
    def _():
        cin[...] = jnp.zeros_like(cin)

    for k in range(1, 4):
        @pl.when(sec > 3 - k)
        def _():
            xin[k - 1] = jnp.zeros_like(xin[k - 1])

    def chain(n):
        for m in range(M):
            for du in range(1, 4):
                r3[m, n, du].copy.wait_recv()
                r3[m, n, du].received = True

            @pl.when(sec < 3)
            def _():
                ch[n, m].wait_recv()

            total = pown[m, n, 0:T] + cin[n, m].astype(F32)
            for du in range(1, 4):
                total = total + sin[m, n, du - 1].astype(F32)
            csend[n, m] = total.astype(BF16)

            @pl.when(sec > 0)
            def _():
                ch[n, m].start()

            cut = pl.ds(n * CW, CW)
            rstage[m, :, cut] = (tv[m, :, cut].astype(F32) + total).astype(BF16)

    def chain_on(section, n):
        @pl.when(sec == section)
        def _():
            chain(n)

    def last_terms():
        n = NC - 1
        for m in range(M):
            r2[m, n].wait_recv()
            total = pown[m, n, 0:T] + rin[m, n, 0:T].astype(F32)
            csend[n, m] = total.astype(BF16)
            pown[m, n, 0:T] = total
            for k in range(1, 4):
                @pl.when(sec >= k)
                def _():
                    last[k, m].start()

    def last_sums():
        n = NC - 1
        cut = pl.ds(n * CW, CW)
        for m in range(M):
            total = tv[m, :, cut].astype(F32) + pown[m, n, 0:T]
            for k in range(1, 4):
                @pl.when(sec <= 3 - k)
                def _():
                    last[k, m].wait_recv()
                total = total + xin[k - 1, m].astype(F32)
            rstage[m, :, cut] = total.astype(BF16)

    def gathered_all():
        for m in range(M):
            for zz in range(2):
                for side in range(2):
                    tf[m, zz, side].wait_recv()

    plan = [(combine, 0), (combine, 1), (spread, 0), (combine, 2), (gathered_all,), (send_rows, 0), (chain_on, 3, 0),
            (spread, 1), (combine, 3), (send_rows, 1), (chain_on, 3, 1), (chain_on, 2, 0), (spread, 2), (spread, 3),
            (send_rows, 2), (chain_on, 3, 2), (chain_on, 2, 1), (chain_on, 1, 0), (send_rows, 3), (last_terms,),
            (chain_on, 0, 0), (chain_on, 1, 1), (chain_on, 2, 2), (weights, 0), (chain_on, 0, 1), (weights, 1),
            (chain_on, 1, 2), (weights, 2), (chain_on, 0, 2), (last_sums,), (weights, 3)]
    for step, *at in plan:
        step(*at)

    out_r = pltpu.make_async_copy(rstage, resid, lsem.at[5])
    out_r.start()
    for cp in started:
        cp.wait_recv()
        cp.wait_send()

    @pl.when(sec > 0)
    def _():
        for at in ch:
            ch[at].wait_send()

    for k in range(1, 4):
        @pl.when(sec >= k)
        def _():
            for m in range(M):
                last[k, m].wait_send()

    for n in outs:
        if n + 2 not in outs:
            for cp in outs[n]:
                cp.wait()
    out_r.wait()


def fused(act, routes, gates, hcot, wgt, top):
    hbm = pl.BlockSpec(memory_space=pl.ANY)
    vmem = pl.BlockSpec(memory_space=pltpu.VMEM)
    sem = pltpu.SemaphoreType.DMA
    v = pltpu.VMEM
    pairs = [M, M * 7, M * 7, M * 4, M * 4, M * 7, M * NC * 7, M * NC, M * NC * 3, M * NC * 7, M * (NC - 1), M * 3]
    sems = [sem((6,)), sem((4,))]
    for n in pairs:
        sems += [sem((n,)), sem((n,))]
    return pl.pallas_call(
        kernel,
        out_shape=(
            jax.ShapeDtypeStruct((D, F), BF16),
            jax.ShapeDtypeStruct((D, F), BF16),
            jax.ShapeDtypeStruct((M, T, D), BF16),
        ),
        in_specs=[hbm, vmem, vmem, hbm, hbm, hbm],
        out_specs=(hbm, hbm, hbm),
        scratch_shapes=[
            v((M, NB, 16, 128), BF16),
            v((M, NB, T, 128), BF16),
            v((M, NB, T, D), BF16),
            v((M, NI * ROWS, NB * T), BF16),
            v((M, NB * T, NI * ROWS), BF16),
            v((M, 16, 128), BF16),
            v((M, NI, 16, 128), BF16),
            v((F, F), BF16),
            v((M, F, F), BF16),
            v((D, F), BF16),
            v((M, T, D), BF16),
            v((M, NI * ROWS, F), BF16),
            v((M, NC, NI * ROWS, CW), BF16),
            v((M, NC, NI * ROWS, CW), BF16),
            v((M, NC, NI * ROWS, CW), BF16),
            v((M, NC, 4 * T, CW), F32),
            v((M, NC, 4 * T, CW), BF16),
            v((M, NC, 4 * T, CW), BF16),
            v((M, NC - 1, 3, T, CW), BF16),
            v((M, NC - 1, 3, T, CW), BF16),
            v((M, 3, 2, T, CW), BF16),
            v((M, 3, 2, T, CW), BF16),
            v((NC, M, T, CW), BF16),
            v((NC - 1, M, T, CW), BF16),
            v((3, M, T, CW), BF16),
            v((M, T, D), BF16),
            v((2, CW, F), BF16),
            v((2, CW, F), BF16),
        ] + sems,
        compiler_params=pltpu.CompilerParams(
            collective_id=0, has_side_effects=True, vmem_limit_bytes=62 * 2**20),
        cost_estimate=pl.CostEstimate(flops=18 * 10**9, bytes_accessed=26 * 10**6, transcendentals=0),
        name="expert_backward",
    )(act, routes, gates, hcot, wgt, top)


def hand_on(grad, fish, resid, grad_out, fish_out, resid_out, gbuf, fbuf, rbuf, in_sems, out_sems):
    cuts = [pl.ds(n * CW, CW) for n in range(NC)]
    ways = []
    for cut in cuts:
        ways.append((grad.at[cut], gbuf.at[cut], grad_out.at[cut]))
        ways.append((fish.at[cut], fbuf.at[cut], fish_out.at[cut]))
    ways.append((resid, rbuf, resid_out))
    loads = [pltpu.make_async_copy(a, b, in_sems.at[k]) for k, (a, b, _) in enumerate(ways)]
    stores = [pltpu.make_async_copy(b, c, out_sems.at[k]) for k, (_, b, c) in enumerate(ways)]
    for cp in loads:
        cp.start()
    for load, store in zip(loads, stores):
        load.wait()
        store.start()
    for cp in stores:
        cp.wait()


def handed_on(*arrays):
    hbm = pl.BlockSpec(memory_space=pl.ANY)
    return pl.pallas_call(
        hand_on,
        out_shape=tuple(jax.ShapeDtypeStruct(a.shape, a.dtype) for a in arrays),
        in_specs=[hbm] * 3,
        out_specs=(hbm,) * 3,
        scratch_shapes=[pltpu.VMEM(a.shape, a.dtype) for a in arrays]
        + [pltpu.SemaphoreType.DMA((2 * NC + 1,))] * 2,
        compiler_params=pltpu.CompilerParams(vmem_limit_bytes=60 * 2**20),
        name="results",
    )(*arrays)


def shards(activations, routes, gates, hidden_cot, weight, top_cot):
    grad, fish, resid = fused(
        activations[0], jnp.swapaxes(routes[0], 1, 2), jnp.swapaxes(gates[0], 1, 2), hidden_cot[0, :, 0], weight[0, 0], top_cot)
    grad, fish, resid = handed_on(grad, fish, resid)
    return grad[None, None], fish[None, None], resid[None]


def solution(mesh):
    return jax.shard_map(
        shards,
        mesh=mesh,
        in_specs=(
            P("section", None, "dp", None),
            P("section", None, "dp", None),
            P("section", None, "dp", None),
            P("section", None, "dp", None, None),
            P("section", "dp", None, None),
            P(None, "dp", None),
        ),
        out_specs=(
            P("section", "dp", None, None),
            P("section", "dp", None, None),
            P("section", None, "dp", None),
        ),
        check_vma=False,
    )
```
